512 devices in a mesh: ctx: 16 (over z, x_lo), ch: 32 (over x_hi, y, core).
Axes of the slice: x: 4 (x_hi: 2, x_lo: 2; x = x_hi * 2 + x_lo), y: 8, z: 8, core: 2. Of those that a mesh axis runs over, the one named last changes fastest.
Arguments:
- hidden: bfloat16 [4096, 4096], P('ctx', 'ch'), may hold values from -6 to 6
- token_ids: int32 [4096], P('ctx'), may hold values from 0 to 11
- embedding: bfloat16 [12, 4096], P(None, 'ch'), may hold values from -6 to 6
- filters: bfloat16 [16, 256], replicated, may hold values from -0.5 to 0.5
- lengths: int32 [16], replicated, may hold values from 1 to 8, as said below
- cotangent: bfloat16 [4096, 4096], P('ctx', 'ch'), may hold values from -6 to 6
Outputs:
- mixed: bfloat16 [4096, 4096], P('ctx', 'ch')
- hidden_grad: bfloat16 [4096, 4096], P('ctx', 'ch')
- filter_grad: float32 [16, 256], replicated
The draws below stay inside these ranges and needn't reach their ends.
Inputs may be any that keep to these rules, and one draw needn't show every extreme that they name: Group g's filter keeps its first 32 * lengths[g] taps; in every draw two groups have 8 blocks and one group has 1. `token_ids`: a symbol of the vocabulary.
All inputs are finite; a program needn't handle non-finite values.
Results may differ from the reference program's by a relative error of at most 0.0051.
Values may be sent and summed in bfloat16 or wider, within the bound.
No kernel may reach another device: no remote copies, remote signals or barrier semaphores. Data moves between devices by JAX's collectives and lax.ppermute only.
A program may use at most 64 MiB of HBM per device.

```python
import math
import jax
import jax.numpy as jnp
from jax import lax

D = 4096
GW = 256
VOCAB = 12
NBMAX = 8
G = 16
BT = 32
KMAX = 256
TOKENS = 4096


def draw_lengths(key, part):
    short_key = jax.random.fold_in(key, 11)
    order_key = jax.random.fold_in(key, 12)
    counts_drawn = jax.random.randint(short_key, (G,), 1, 5)
    shuffled = jax.random.permutation(order_key, G)
    counts_drawn = counts_drawn.at[shuffled[0]].set(NBMAX)
    counts_drawn = counts_drawn.at[shuffled[1]].set(NBMAX)
    counts_drawn = counts_drawn.at[shuffled[2]].set(1)
    return counts_drawn.astype(jnp.int32)


def set_ends(values, own_key, least, top_value):
    longest = values.shape.index(max(values.shape))
    spots = []
    for shift in (0, 1):
        where = [jax.random.randint(jax.random.fold_in(own_key, axis), (), 0, length) for axis, length in enumerate(values.shape)]
        where[longest] = (where[longest] + shift) % values.shape[longest]
        spots.append(tuple(where))
    return values.at[spots[0]].set(least).at[spots[1]].set(top_value)


def levels(own_key, extent, pieces, smallest, high):
    level = 1.0
    for axis_at, shards_of in pieces:
        heights = jax.random.uniform(jax.random.fold_in(jax.random.fold_in(own_key, 6), axis_at), (shards_of,), jnp.float32, smallest / len(pieces), high / len(pieces))
        level = level * jnp.repeat(jnp.exp(heights), extent[axis_at] // shards_of).reshape((-1,) + (1,) * (len(extent) - 1 - axis_at))
    return level


def centred(rng, extent, spread, limit, cuts=(), held_as=jnp.bfloat16):
    gain = levels(rng, extent, cuts, -0.22, 0.18) if cuts else 1.0
    values = jax.random.normal(rng, extent, jnp.float32) * spread * gain
    return jnp.minimum(jnp.maximum(values, -limit), limit).astype(held_as)


def setup_inputs(seed: int = 0) -> dict:
    streams_of = jax.random.split(jax.random.key(seed), 7)
    hidden = centred(streams_of[0], (TOKENS, D), 1.0, 6.0, ((0, 16), (1, 32)))
    token_ids = set_ends(jax.random.randint(streams_of[1], (TOKENS,), 0, VOCAB), jax.random.fold_in(streams_of[1], 1), 0, VOCAB - 1).astype(jnp.int32)
    embedding = centred(streams_of[2], (VOCAB, D), 1.0, 6.0, ((1, 32),))
    filters = centred(streams_of[3], (G, KMAX), (KMAX // 2) ** -0.5, 0.5)
    lengths = draw_lengths(jax.random.fold_in(streams_of[6], 71), 0)
    cotangent = centred(streams_of[5], (TOKENS, D), 1.0, 6.0, ((0, 16), (1, 32)))
    return {"hidden": hidden, "token_ids": token_ids, "embedding": embedding, "filters": filters, "lengths": lengths, "cotangent": cotangent}


def grouped_conv(values, taps_all):
    seq_len = values.shape[0]
    size_fft = seq_len + taps_all.shape[1]
    split = values.reshape(seq_len, G, GW).transpose(1, 0, 2)

    def one_group(pair_in):
        block, taps_one = pair_in
        spec_in = jnp.fft.rfft(block, n=size_fft, axis=0)
        spec_taps = jnp.fft.rfft(taps_one, n=size_fft)
        return jnp.fft.irfft(spec_in * spec_taps[:, None], n=size_fft, axis=0)[:seq_len]
    result = lax.map(one_group, (split, taps_all))
    return result.transpose(1, 0, 2).reshape(seq_len, D)

def layer_map(values, taps_all):
    forward = grouped_conv(values, taps_all)
    reverse = grouped_conv(values[::-1, ::-1], taps_all)[::-1, ::-1]
    return forward + reverse

def reference(hidden, token_ids, embedding, filters, lengths, cotangent):
    onehot = (token_ids[:, None] == jnp.arange(VOCAB, dtype=jnp.int32)[None, :]).astype(jnp.float32)
    looked = jnp.dot(onehot, embedding.astype(jnp.float32), precision=lax.Precision.HIGHEST, preferred_element_type=jnp.float32)
    rounded = (hidden.astype(jnp.float32) + looked).astype(jnp.bfloat16)
    rounded = lax.optimization_barrier(rounded)
    inputs = rounded.astype(jnp.float32)
    tap_mask = jnp.arange(KMAX, dtype=jnp.int32)[None, :] < (lengths * BT)[:, None]
    taps_all = jnp.where(tap_mask, filters.astype(jnp.float32), jnp.float32(0.0))
    mixed, pullback = jax.vjp(layer_map, inputs, taps_all)
    grad_inputs, grad_taps = pullback(cotangent.astype(jnp.float32))
    scale = 1.0 / math.sqrt(TOKENS * GW)
    filter_grad = jnp.where(tap_mask, grad_taps * scale, jnp.float32(0.0))
    return (mixed.astype(jnp.bfloat16), grad_inputs.astype(jnp.bfloat16), filter_grad.astype(jnp.float32))
```

```python
import math

import jax
import jax.numpy as jnp
from jax import lax
from jax.experimental import pallas as pl
from jax.experimental.pallas import tpu as pltpu
from jax.sharding import Mesh, PartitionSpec as P

GW = 256
BT = 32
ROWS = 256
CHANS = 128
TAPS = 256
GROUPS = 16
PARTS = (("z", 8), ("x_lo", 2), ("x_hi", 2), ("y", 8), ("core", 2))
CTX = ("z", "x_lo")
GROUP = ("x_hi", "y")
SUMMED = ("z", "x_lo", "core")
CTX_SIZE = 16
SUMMED_SIZE = 32

VMEM = pl.BlockSpec(memory_space=pltpu.VMEM)
SMEM = pl.BlockSpec(memory_space=pltpu.SMEM)


def dot(a, b, contract):
    return lax.dot_general(a, b, (contract, ((), ())), preferred_element_type=jnp.float32)


def cost(flops, moved):
    return pl.CostEstimate(flops=flops, bytes_accessed=moved, transcendentals=0)


ROOM = pltpu.CompilerParams(vmem_limit_bytes=16 * 1024 * 1024)


def iota(shape, dim):
    return lax.broadcasted_iota(jnp.int32, shape, dim)


def inputs_kernel(hidden, ids, table, cotangent, both):
    symbols = table.shape[0]
    shape = (symbols, ROWS)
    ids_row = jnp.broadcast_to(ids[...].reshape(1, ROWS), shape)
    onehot = jnp.where(iota(shape, 0) == ids_row, 1.0, 0.0)
    looked = dot(onehot, table[...].astype(jnp.float32), ((0,), (0,)))
    both[0] = (hidden[...].astype(jnp.float32) + looked).astype(jnp.bfloat16)
    both[1] = cotangent[...]


def lag_sums(product):
    half = ROWS // 2
    while half >= 8:
        product = product[:half] + pltpu.roll(product[half:], TAPS - half, 1)
        half //= 2
    row = iota(product.shape, 0)
    for step in (4, 2, 1):
        product = jnp.where((row & step) != 0, pltpu.roll(product, TAPS - step, 1), product)
    return jnp.sum(product, axis=0, keepdims=True)


def correlate_kernel(both, left, out):
    shape = (ROWS, ROWS)
    here = iota(shape, 1) >= iota(shape, 0)
    lane = ((1,), (1,))
    sums = []
    for first, second in ((0, 1), (1, 0)):
        fixed = both[second]
        near = dot(both[first], fixed, lane)
        far = dot(left[first], fixed, lane)
        sums.append(lag_sums(jnp.where(here, near, far)))
    half = TAPS // 2
    pieces = [sums[0][:, :half], sums[0][:, half:], sums[1][:, :half], sums[1][:, half:]]
    row = iota((4, half), 0)
    packed = jnp.where(row < 2, jnp.where(row == 0, pieces[0], pieces[1]),
                       jnp.where(row == 2, pieces[2], pieces[3]))
    for peer in range(out.shape[0]):
        out[peer] = packed


def sum_kernel(parts, out):
    total = jnp.sum(parts[...], axis=0)
    for peer in range(out.shape[0]):
        out[peer] = total


def finish_kernel(parts, factor, out):
    half = TAPS // 2
    for group in range(GROUPS):
        own = parts[group]
        other = parts[GROUPS - 1 - group]
        out[group : group + 1, :half] = own[0:1] + other[2:3]
        out[group : group + 1, half:] = own[1:2] + other[3:4]
    scaled = factor[...]
    out[...] = jnp.where(scaled != 0.0, out[...] * scaled, 0.0)


def outputs_kernel(both, left, right, filters, lengths, mixed, grad, factor):
    taps_shape = (GROUPS, TAPS)
    group_row = iota(taps_shape, 0)
    tap_lane = iota(taps_shape, 1)
    reach = jnp.zeros(taps_shape, jnp.int32)
    for group in range(GROUPS):
        reach = jnp.where(group_row == group, lengths[group] * BT, reach)
    kept = tap_lane < reach
    scale = 1.0 / math.sqrt(ROWS * CTX_SIZE * GW)
    factor[...] = jnp.where(kept, scale, 0.0)
    taps = jnp.where(kept, filters[...].astype(jnp.float32), 0.0)
    mine = lax.axis_index("x_hi") * 8 + lax.axis_index("y")

    def circulant(index):
        row = jnp.sum(jnp.where(group_row == index, taps, 0.0), axis=0, keepdims=True)
        spread = pltpu.roll(jnp.broadcast_to(row, (ROWS, TAPS)), 0, 1, stride=1, stride_axis=0)
        return row[:, :1], spread, spread.T

    own_first, own, own_t = circulant(mine)
    other_first, other, other_t = circulant(GROUPS - 1 - mine)
    shape = (ROWS, ROWS)
    row, lane = iota(shape, 0), iota(shape, 1)
    below = row > lane
    above = row < lane

    def matrix(mask, yes, no):
        return jnp.where(mask, yes, no).astype(jnp.bfloat16)

    plain = ((1,), (0,))
    inputs, cotangent = both[0], both[1]
    total = dot(matrix(below, own_t, other), inputs, plain)
    total += dot(matrix(above, own_t, 0.0), left[0], plain)
    total += dot(matrix(below, other, 0.0), right[0], plain)
    mixed[...] = (total + own_first * inputs.astype(jnp.float32)).astype(jnp.bfloat16)
    total = dot(matrix(below, other_t, own), cotangent, plain)
    total += dot(matrix(below, own, 0.0), right[1], plain)
    total += dot(matrix(above, other_t, 0.0), left[1], plain)
    grad[...] = (total + other_first * cotangent.astype(jnp.float32)).astype(jnp.bfloat16)


def on_device(hidden, token_ids, embedding, filters, lengths, cotangent):
    shape = jax.ShapeDtypeStruct
    half = TAPS // 2
    both = pl.pallas_call(
        inputs_kernel,
        out_shape=shape((2, ROWS, CHANS), jnp.bfloat16),
        in_specs=[VMEM] * 4,
        out_specs=VMEM,
        cost_estimate=cost(2 * 16 * ROWS * CHANS, 1 << 18),
    )(hidden, token_ids, embedding, cotangent)
    up = [(i, i + 1) for i in range(CTX_SIZE - 1)]
    left = lax.ppermute(both, CTX, up)
    right = lax.ppermute(both, CTX, [(j, i) for i, j in up])
    sums = pl.pallas_call(
        correlate_kernel,
        out_shape=shape((SUMMED_SIZE, 4, half), jnp.float32),
        in_specs=[VMEM] * 2,
        out_specs=VMEM,
        cost_estimate=cost(8 * ROWS * ROWS * CHANS, 1 << 18),
        compiler_params=ROOM,
    )(both, left)
    sums = lax.all_to_all(sums, SUMMED, 0, 0)
    sums = pl.pallas_call(
        sum_kernel,
        out_shape=shape((GROUPS, 4, half), jnp.float32),
        in_specs=[VMEM],
        out_specs=VMEM,
        cost_estimate=cost(1 << 16, 1 << 17),
        compiler_params=ROOM,
    )(sums)
    sums = lax.all_to_all(sums, GROUP, 0, 0)
    block = shape((ROWS, CHANS), jnp.bfloat16)
    mixed, hidden_grad, factor = pl.pallas_call(
        outputs_kernel,
        out_shape=(block, block, shape((GROUPS, TAPS), jnp.float32)),
        in_specs=[VMEM] * 4 + [SMEM],
        out_specs=(VMEM,) * 3,
        cost_estimate=cost(12 * ROWS * ROWS * CHANS, 1 << 19),
        compiler_params=ROOM,
    )(both, left, right, filters, lengths)
    filter_grad = pl.pallas_call(
        finish_kernel,
        out_shape=shape((GROUPS, TAPS), jnp.float32),
        in_specs=[VMEM] * 2,
        out_specs=VMEM,
        cost_estimate=cost(1 << 14, 1 << 16),
        compiler_params=ROOM,
    )(sums, factor)
    return mixed, hidden_grad, filter_grad


def solution(mesh):
    names = tuple(name for name, _ in PARTS)
    fine = Mesh(mesh.devices.reshape([size for _, size in PARTS]), names)
    ctx, ch = names[:2], names[2:]
    placed = (P(ctx, ch), P(ctx), P(None, ch), P(), P(), P(ctx, ch))
    return jax.shard_map(
        on_device,
        mesh=fine,
        in_specs=placed,
        out_specs=(P(ctx, ch), P(ctx, ch), P()),
        check_vma=False,
    )
```

```python
import math

import jax
import jax.numpy as jnp
from jax import lax
from jax.experimental import pallas as pl
from jax.experimental.pallas import tpu as pltpu
from jax.sharding import Mesh, PartitionSpec as P

GW = 256
BT = 32
ROWS = 256
CHANS = 128
TAPS = 256
GROUPS = 16
PARTS = (("z", 8), ("x_lo", 2), ("x_hi", 2), ("y", 8), ("core", 2))
CTX = ("z", "x_lo")
GROUP = ("x_hi", "y")
SUMMED = ("z", "x_lo", "core")
CTX_SIZE = 16
SUMMED_SIZE = 32

VMEM = pl.BlockSpec(memory_space=pltpu.VMEM)
SMEM = pl.BlockSpec(memory_space=pltpu.SMEM)


def dot(a, b, contract):
    return lax.dot_general(a, b, (contract, ((), ())), preferred_element_type=jnp.float32)


def cost(flops, moved):
    return pl.CostEstimate(flops=flops, bytes_accessed=moved, transcendentals=0)


ROOM = pltpu.CompilerParams(vmem_limit_bytes=16 * 1024 * 1024)


def iota(shape, dim):
    return lax.broadcasted_iota(jnp.int32, shape, dim)


def inputs_kernel(hidden, ids, table, inputs):
    symbols = table.shape[0]
    shape = (symbols, ROWS)
    ids_row = jnp.broadcast_to(ids[...].reshape(1, ROWS), shape)
    onehot = jnp.where(iota(shape, 0) == ids_row, 1.0, 0.0)
    looked = dot(onehot, table[...].astype(jnp.float32), ((0,), (0,)))
    inputs[...] = (hidden[...].astype(jnp.float32) + looked).astype(jnp.bfloat16)


def lag_sums(product):
    half = ROWS // 2
    while half >= 8:
        product = product[:half] + pltpu.roll(product[half:], TAPS - half, 1)
        half //= 2
    row = iota(product.shape, 0)
    for step in (4, 2, 1):
        product = jnp.where((row & step) != 0, pltpu.roll(product, TAPS - step, 1), product)
    return jnp.sum(product, axis=0, keepdims=True)


def correlate_kernel(inputs, cotangent, left, right, out):
    shape = (ROWS, ROWS)
    here = iota(shape, 1) >= iota(shape, 0)
    lane = ((1,), (1,))
    source, grads = inputs[...], cotangent[...]
    own = jnp.where(here, dot(source, grads, lane), dot(source, right[...], lane))
    other = jnp.where(here, dot(grads, source, lane), dot(left[...], source, lane))
    sums = [lag_sums(own), lag_sums(other)]
    half = TAPS // 2
    pieces = [sums[0][:, :half], sums[0][:, half:], sums[1][:, :half], sums[1][:, half:]]
    row = iota((4, half), 0)
    packed = jnp.where(row < 2, jnp.where(row == 0, pieces[0], pieces[1]),
                       jnp.where(row == 2, pieces[2], pieces[3]))
    for peer in range(out.shape[0]):
        out[peer] = packed


def sum_kernel(parts, out):
    total = jnp.sum(parts[...], axis=0)
    for peer in range(out.shape[0]):
        out[peer] = total


def finish_kernel(parts, factor, out):
    half = TAPS // 2
    for group in range(GROUPS):
        own = parts[group]
        other = parts[GROUPS - 1 - group]
        out[group : group + 1, :half] = own[0:1] + other[2:3]
        out[group : group + 1, half:] = own[1:2] + other[3:4]
    scaled = factor[...]
    out[...] = jnp.where(scaled != 0.0, out[...] * scaled, 0.0)


def outputs_kernel(inputs, cotangent, in_left, in_right, ct_left, ct_right, filters, lengths, mixed, grad, factor):
    taps_shape = (GROUPS, TAPS)
    group_row = iota(taps_shape, 0)
    tap_lane = iota(taps_shape, 1)
    reach = jnp.zeros(taps_shape, jnp.int32)
    for group in range(GROUPS):
        reach = jnp.where(group_row == group, lengths[group] * BT, reach)
    kept = tap_lane < reach
    scale = 1.0 / math.sqrt(ROWS * CTX_SIZE * GW)
    factor[...] = jnp.where(kept, scale, 0.0)
    taps = jnp.where(kept, filters[...].astype(jnp.float32), 0.0)
    mine = lax.axis_index("x_hi") * 8 + lax.axis_index("y")

    def circulant(index):
        row = jnp.sum(jnp.where(group_row == index, taps, 0.0), axis=0, keepdims=True)
        spread = pltpu.roll(jnp.broadcast_to(row, (ROWS, TAPS)), 0, 1, stride=1, stride_axis=0)
        return row[:, :1], spread, spread.T

    own_first, own, own_t = circulant(mine)
    other_first, other, other_t = circulant(GROUPS - 1 - mine)
    shape = (ROWS, ROWS)
    row, lane = iota(shape, 0), iota(shape, 1)
    below = row > lane
    above = row < lane

    def matrix(mask, yes, no):
        return jnp.where(mask, yes, no).astype(jnp.bfloat16)

    plain = ((1,), (0,))
    source, grads = inputs[...], cotangent[...]
    total = dot(matrix(below, own_t, other), source, plain)
    total += dot(matrix(above, own_t, 0.0), in_left[...], plain)
    total += dot(matrix(below, other, 0.0), in_right[...], plain)
    mixed[...] = (total + own_first * source.astype(jnp.float32)).astype(jnp.bfloat16)
    total = dot(matrix(below, other_t, own), grads, plain)
    total += dot(matrix(below, own, 0.0), ct_right[...], plain)
    total += dot(matrix(above, other_t, 0.0), ct_left[...], plain)
    grad[...] = (total + other_first * grads.astype(jnp.float32)).astype(jnp.bfloat16)


def on_device(hidden, token_ids, embedding, filters, lengths, cotangent):
    shape = jax.ShapeDtypeStruct
    half = TAPS // 2
    up = [(i, i + 1) for i in range(CTX_SIZE - 1)]
    down = [(j, i) for i, j in up]
    ct_left = lax.ppermute(cotangent, CTX, up)
    ct_right = lax.ppermute(cotangent, CTX, down)
    block = shape((ROWS, CHANS), jnp.bfloat16)
    inputs = pl.pallas_call(
        inputs_kernel,
        out_shape=block,
        in_specs=[VMEM] * 3,
        out_specs=VMEM,
        cost_estimate=cost(2 * 16 * ROWS * CHANS, 1 << 18),
        compiler_params=ROOM,
    )(hidden, token_ids, embedding)
    sums = pl.pallas_call(
        correlate_kernel,
        out_shape=shape((SUMMED_SIZE, 4, half), jnp.float32),
        in_specs=[VMEM] * 4,
        out_specs=VMEM,
        cost_estimate=cost(8 * ROWS * ROWS * CHANS, 1 << 18),
        compiler_params=ROOM,
    )(inputs, cotangent, ct_left, ct_right)
    sums, late_inputs = lax.optimization_barrier((sums, inputs))
    in_left = lax.ppermute(late_inputs, CTX, up)
    in_right = lax.ppermute(late_inputs, CTX, down)
    sums = lax.all_to_all(sums, SUMMED, 0, 0)
    sums = pl.pallas_call(
        sum_kernel,
        out_shape=shape((GROUPS, 4, half), jnp.float32),
        in_specs=[VMEM],
        out_specs=VMEM,
        cost_estimate=cost(1 << 16, 1 << 17),
        compiler_params=ROOM,
    )(sums)
    sums = lax.all_to_all(sums, GROUP, 0, 0)
    mixed, hidden_grad, factor = pl.pallas_call(
        outputs_kernel,
        out_shape=(block, block, shape((GROUPS, TAPS), jnp.float32)),
        in_specs=[VMEM] * 7 + [SMEM],
        out_specs=(VMEM,) * 3,
        cost_estimate=cost(12 * ROWS * ROWS * CHANS, 1 << 19),
        compiler_params=ROOM,
    )(inputs, cotangent, in_left, in_right, ct_left, ct_right, filters, lengths)
    filter_grad = pl.pallas_call(
        finish_kernel,
        out_shape=shape((GROUPS, TAPS), jnp.float32),
        in_specs=[VMEM] * 2,
        out_specs=VMEM,
        cost_estimate=cost(1 << 14, 1 << 16),
        compiler_params=ROOM,
    )(sums, factor)
    return mixed, hidden_grad, filter_grad


def solution(mesh):
    names = tuple(name for name, _ in PARTS)
    fine = Mesh(mesh.devices.reshape([size for _, size in PARTS]), names)
    ctx, ch = names[:2], names[2:]
    placed = (P(ctx, ch), P(ctx), P(None, ch), P(), P(), P(ctx, ch))
    return jax.shard_map(
        on_device,
        mesh=fine,
        in_specs=placed,
        out_specs=(P(ctx, ch), P(ctx, ch), P()),
        check_vma=False,
    )
```

```python
import math

import jax
import jax.numpy as jnp
from jax import lax
from jax.experimental import pallas as pl
from jax.experimental.pallas import tpu as pltpu
from jax.sharding import Mesh, PartitionSpec as P

GW = 256
BT = 32
ROWS = 256
CHANS = 128
TAPS = 256
GROUPS = 16
PARTS = (("z", 8), ("x_lo", 2), ("x_hi", 2), ("y", 8), ("core", 2))
CTX = ("z", "x_lo")
FIRST = ("core","z")
SECOND = ("x_lo","x_hi","y")
SIZES = dict(PARTS)
CTX_SIZE = 16

VMEM = pl.BlockSpec(memory_space=pltpu.VMEM)
SMEM = pl.BlockSpec(memory_space=pltpu.SMEM)


def dot(a, b, contract):
    return lax.dot_general(a, b, (contract, ((), ())), preferred_element_type=jnp.float32)


def cost(flops, moved):
    return pl.CostEstimate(flops=flops, bytes_accessed=moved, transcendentals=0)


ROOM = pltpu.CompilerParams(vmem_limit_bytes=16 * 1024 * 1024)


def iota(shape, dim):
    return lax.broadcasted_iota(jnp.int32, shape, dim)


def inputs_kernel(hidden, ids, table, cotangent, both):
    symbols = table.shape[0]
    shape = (symbols, ROWS)
    ids_row = jnp.broadcast_to(ids[...].reshape(1, ROWS), shape)
    onehot = jnp.where(iota(shape, 0) == ids_row, 1.0, 0.0)
    looked = dot(onehot, table[...].astype(jnp.float32), ((0,), (0,)))
    both[0] = (hidden[...].astype(jnp.float32) + looked).astype(jnp.bfloat16)
    both[1] = cotangent[...]


def lag_sums(product):
    half = ROWS // 2
    while half >= 8:
        product = product[:half] + pltpu.roll(product[half:], TAPS - half, 1)
        half //= 2
    row = iota(product.shape, 0)
    for step in (4, 2, 1):
        product = jnp.where((row & step) != 0, pltpu.roll(product, TAPS - step, 1), product)
    return jnp.sum(product, axis=0, keepdims=True)


LANE = ((1,), (1,))


def lag_here():
    shape = (ROWS, ROWS)
    return iota(shape, 1) >= iota(shape, 0)


def near_kernel(both, near):
    here = lag_here()
    for first, second in ((0, 1), (1, 0)):
        near[first] = jnp.where(here, dot(both[first], both[second], LANE), 0.0)


def correlate_kernel(both, right, near, out):
    here = lag_here()
    sums = []
    for first, second in ((0, 1), (1, 0)):
        far = dot(both[first], right[second], LANE)
        sums.append(lag_sums(jnp.where(here, near[first], far)))
    half = TAPS // 2
    pieces = [sums[0][:, :half], sums[0][:, half:], sums[1][:, :half], sums[1][:, half:]]
    row = iota((4, half), 0)
    packed = jnp.where(row < 2, jnp.where(row == 0, pieces[0], pieces[1]),
                       jnp.where(row == 2, pieces[2], pieces[3]))
    for peer in range(out.shape[0]):
        out[peer] = packed


def sources(axes, fixed):
    places = [0]
    for name in axes:
        size = SIZES[name]
        picks = [fixed[name]] if name in fixed else range(size)
        places = [place * size + pick for place in places for pick in picks]
    return places


def tree_sum(terms):
    while len(terms) > 1:
        terms = [sum(terms[i : i + 2][1:], terms[i]) for i in range(0, len(terms), 2)]
    return terms[0]


def kept_places():
    places = [{}]
    for name in FIRST:
        if name in ("x_hi", "y"):
            places = [dict(place, **{name: i}) for place in places for i in range(SIZES[name])]
    return places


def sum_kernel(parts, out):
    for kept, fixed in enumerate(kept_places()):
        total = tree_sum([parts[place] for place in sources(FIRST, fixed)])
        for peer in range(out.shape[0]):
            out[peer, kept] = total


def group_sum(parts, group):
    coords = {"x_hi": group // 8, "y": group % 8}
    kept = next(i for i, fixed in enumerate(kept_places()) if fixed.items() <= coords.items())
    return tree_sum([parts[place, kept] for place in sources(SECOND, coords)])


def finish_kernel(parts, factor, out):
    half = TAPS // 2
    total = [group_sum(parts, group) for group in range(GROUPS)]
    for group in range(GROUPS):
        own = total[group]
        other = total[GROUPS - 1 - group]
        out[group : group + 1, :half] = own[0:1] + other[2:3]
        out[group : group + 1, half:] = own[1:2] + other[3:4]
    scaled = factor[...]
    out[...] = jnp.where(scaled != 0.0, out[...] * scaled, 0.0)


def outputs_kernel(both, left, right, filters, lengths, mixed, grad, factor):
    taps_shape = (GROUPS, TAPS)
    group_row = iota(taps_shape, 0)
    tap_lane = iota(taps_shape, 1)
    reach = jnp.zeros(taps_shape, jnp.int32)
    for group in range(GROUPS):
        reach = jnp.where(group_row == group, lengths[group] * BT, reach)
    kept = tap_lane < reach
    scale = 1.0 / math.sqrt(ROWS * CTX_SIZE * GW)
    factor[...] = jnp.where(kept, scale, 0.0)
    taps = jnp.where(kept, filters[...].astype(jnp.float32), 0.0)
    mine = lax.axis_index("x_hi") * 8 + lax.axis_index("y")

    def circulant(index):
        row = jnp.sum(jnp.where(group_row == index, taps, 0.0), axis=0, keepdims=True)
        spread = pltpu.roll(jnp.broadcast_to(row, (ROWS, TAPS)), 0, 1, stride=1, stride_axis=0)
        return row[:, :1], spread, spread.T

    own_first, own, own_t = circulant(mine)
    other_first, other, other_t = circulant(GROUPS - 1 - mine)
    shape = (ROWS, ROWS)
    row, lane = iota(shape, 0), iota(shape, 1)
    below = row > lane
    above = row < lane

    def matrix(mask, yes, no):
        return jnp.where(mask, yes, no).astype(jnp.bfloat16)

    plain = ((1,), (0,))
    inputs, cotangent = both[0], both[1]
    total = dot(matrix(below, own_t, other), inputs, plain)
    total += dot(matrix(above, own_t, 0.0), left[0], plain)
    total += dot(matrix(below, other, 0.0), right[0], plain)
    mixed[...] = (total + own_first * inputs.astype(jnp.float32)).astype(jnp.bfloat16)
    total = dot(matrix(below, other_t, own), cotangent, plain)
    total += dot(matrix(below, own, 0.0), right[1], plain)
    total += dot(matrix(above, other_t, 0.0), left[1], plain)
    grad[...] = (total + other_first * cotangent.astype(jnp.float32)).astype(jnp.bfloat16)


def on_device(hidden, token_ids, embedding, filters, lengths, cotangent):
    shape = jax.ShapeDtypeStruct
    half = TAPS // 2
    both = pl.pallas_call(
        inputs_kernel,
        out_shape=shape((2, ROWS, CHANS), jnp.bfloat16),
        in_specs=[VMEM] * 4,
        out_specs=VMEM,
        cost_estimate=cost(1, 1),
    )(hidden, token_ids, embedding, cotangent)
    up = [(i, i + 1) for i in range(CTX_SIZE - 1)]
    left = lax.ppermute(both, CTX, up)
    right = lax.ppermute(both, CTX, [(j, i) for i, j in up])
    pair = (2, ROWS, ROWS)
    near = pl.pallas_call(
        near_kernel,
        out_shape=shape(pair, jnp.float32),
        in_specs=[VMEM],
        out_specs=VMEM,
        cost_estimate=cost(1, 1),
        compiler_params=ROOM,
    )(both)
    sums = pl.pallas_call(
        correlate_kernel,
        out_shape=shape((math.prod(SIZES[a] for a in FIRST), 4, half), jnp.float32),
        in_specs=[VMEM] * 3,
        out_specs=VMEM,
        cost_estimate=cost(1, 1),
        compiler_params=ROOM,
    )(both, right, near)
    sums = lax.all_to_all(sums, FIRST, 0, 0)
    block = shape((ROWS, CHANS), jnp.bfloat16)
    mixed, hidden_grad, factor = pl.pallas_call(
        outputs_kernel,
        out_shape=(block, block, shape((GROUPS, TAPS), jnp.float32)),
        in_specs=[VMEM] * 4 + [SMEM],
        out_specs=(VMEM,) * 3,
        cost_estimate=cost(1, 1),
        compiler_params=ROOM,
    )(both, left, right, filters, lengths)
    sums, factor = lax.optimization_barrier((sums, factor))
    sums = pl.pallas_call(
        sum_kernel,
        out_shape=shape((math.prod(SIZES[a] for a in SECOND), len(kept_places()), 4, half), jnp.float32),
        in_specs=[VMEM],
        out_specs=VMEM,
        cost_estimate=cost(1, 1),
        compiler_params=ROOM,
    )(sums)
    sums = lax.all_to_all(sums, SECOND, 0, 0)
    filter_grad = pl.pallas_call(
        finish_kernel,
        out_shape=shape((GROUPS, TAPS), jnp.float32),
        in_specs=[VMEM] * 2,
        out_specs=VMEM,
        cost_estimate=cost(1, 1),
        compiler_params=ROOM,
    )(sums, factor)
    return mixed, hidden_grad, filter_grad


def solution(mesh):
    names = tuple(name for name, _ in PARTS)
    fine = Mesh(mesh.devices.reshape([size for _, size in PARTS]), names)
    ctx, ch = names[:2], names[2:]
    placed = (P(ctx, ch), P(ctx), P(None, ch), P(), P(), P(ctx, ch))
    return jax.shard_map(
        on_device,
        mesh=fine,
        in_specs=placed,
        out_specs=(P(ctx, ch), P(ctx, ch), P()),
        check_vma=False,
    )
```

```python
import math

import jax
import jax.numpy as jnp
from jax import lax
from jax.experimental import pallas as pl
from jax.experimental.pallas import tpu as pltpu
from jax.sharding import Mesh, PartitionSpec as P

GW = 256
BT = 32
ROWS = 256
CHANS = 128
TAPS = 256
GROUPS = 16
PARTS = (("z", 8), ("x_lo", 2), ("x_hi", 2), ("y", 8), ("core", 2))
CTX = ("z", "x_lo")
FIRST = ("core","z")
SECOND = ("x_lo","x_hi","y")
SIZES = dict(PARTS)
CTX_SIZE = 16

VMEM = pl.BlockSpec(memory_space=pltpu.VMEM)
SMEM = pl.BlockSpec(memory_space=pltpu.SMEM)


def dot(a, b, contract):
    return lax.dot_general(a, b, (contract, ((), ())), preferred_element_type=jnp.float32)


def cost(flops, moved):
    return pl.CostEstimate(flops=flops, bytes_accessed=moved, transcendentals=0)


ROOM = pltpu.CompilerParams(vmem_limit_bytes=16 * 1024 * 1024)


def iota(shape, dim):
    return lax.broadcasted_iota(jnp.int32, shape, dim)


def symbols_kernel(symbols):
    symbols[...] = iota(symbols.shape, 0)


def inputs_kernel(hidden, ids, table, cotangent, symbols, both):
    ids_row = jnp.broadcast_to(ids[...].reshape(1, ROWS), symbols.shape)
    onehot = jnp.where(symbols[...] == ids_row, 1.0, 0.0)
    looked = dot(onehot, table[...].astype(jnp.float32), ((0,), (0,)))
    both[0] = (hidden[...].astype(jnp.float32) + looked).astype(jnp.bfloat16)
    both[1] = cotangent[...]


def lag_sums(product):
    half = ROWS // 2
    while half >= 8:
        product = product[:half] + pltpu.roll(product[half:], TAPS - half, 1)
        half //= 2
    row = iota(product.shape, 0)
    for step in (4, 2, 1):
        product = jnp.where((row & step) != 0, pltpu.roll(product, TAPS - step, 1), product)
    return jnp.sum(product, axis=0, keepdims=True)


LANE = ((1,), (1,))


def lag_here():
    shape = (ROWS, ROWS)
    return iota(shape, 1) >= iota(shape, 0)


def near_kernel(both, near):
    here = lag_here()
    for first, second in ((0, 1), (1, 0)):
        near[first] = jnp.where(here, dot(both[first], both[second], LANE), 0.0)


def correlate_kernel(both, right, near, out):
    here = lag_here()
    sums = []
    for first, second in ((0, 1), (1, 0)):
        far = dot(both[first], right[second], LANE)
        sums.append(lag_sums(jnp.where(here, near[first], far)))
    half = TAPS // 2
    pieces = [sums[0][:, :half], sums[0][:, half:], sums[1][:, :half], sums[1][:, half:]]
    row = iota((4, half), 0)
    packed = jnp.where(row < 2, jnp.where(row == 0, pieces[0], pieces[1]),
                       jnp.where(row == 2, pieces[2], pieces[3]))
    for peer in range(out.shape[0]):
        out[peer] = packed


def sources(axes, fixed):
    places = [0]
    for name in axes:
        size = SIZES[name]
        picks = [fixed[name]] if name in fixed else range(size)
        places = [place * size + pick for place in places for pick in picks]
    return places


def tree_sum(terms):
    while len(terms) > 1:
        terms = [sum(terms[i : i + 2][1:], terms[i]) for i in range(0, len(terms), 2)]
    return terms[0]


def kept_places():
    places = [{}]
    for name in FIRST:
        if name in ("x_hi", "y"):
            places = [dict(place, **{name: i}) for place in places for i in range(SIZES[name])]
    return places


def sum_kernel(parts, out):
    for kept, fixed in enumerate(kept_places()):
        total = tree_sum([parts[place] for place in sources(FIRST, fixed)])
        for peer in range(out.shape[0]):
            out[peer, kept] = total


def group_sum(parts, group):
    coords = {"x_hi": group // 8, "y": group % 8}
    kept = next(i for i, fixed in enumerate(kept_places()) if fixed.items() <= coords.items())
    return tree_sum([parts[place, kept] for place in sources(SECOND, coords)])


def finish_kernel(parts, factor, out):
    half = TAPS // 2
    total = [group_sum(parts, group) for group in range(GROUPS)]
    for group in range(GROUPS):
        own = total[group]
        other = total[GROUPS - 1 - group]
        out[group : group + 1, :half] = own[0:1] + other[2:3]
        out[group : group + 1, half:] = own[1:2] + other[3:4]
    scaled = factor[...]
    out[...] = jnp.where(scaled != 0.0, out[...] * scaled, 0.0)


def outputs_kernel(both, left, right, filters, lengths, mixed, grad, factor):
    taps_shape = (GROUPS, TAPS)
    group_row = iota(taps_shape, 0)
    tap_lane = iota(taps_shape, 1)
    reach = jnp.zeros(taps_shape, jnp.int32)
    for group in range(GROUPS):
        reach = jnp.where(group_row == group, lengths[group] * BT, reach)
    kept = tap_lane < reach
    scale = 1.0 / math.sqrt(ROWS * CTX_SIZE * GW)
    factor[...] = jnp.where(kept, scale, 0.0)
    taps = jnp.where(kept, filters[...].astype(jnp.float32), 0.0)
    mine = lax.axis_index("x_hi") * 8 + lax.axis_index("y")

    def circulant(index):
        row = jnp.sum(jnp.where(group_row == index, taps, 0.0), axis=0, keepdims=True)
        spread = pltpu.roll(jnp.broadcast_to(row, (ROWS, TAPS)), 0, 1, stride=1, stride_axis=0)
        return row[:, :1], spread, spread.T

    own_first, own, own_t = circulant(mine)
    other_first, other, other_t = circulant(GROUPS - 1 - mine)
    shape = (ROWS, ROWS)
    row, lane = iota(shape, 0), iota(shape, 1)
    below = row > lane
    above = row < lane

    def matrix(mask, yes, no):
        return jnp.where(mask, yes, no).astype(jnp.bfloat16)

    plain = ((1,), (0,))
    inputs, cotangent = both[0], both[1]
    total = dot(matrix(below, own_t, other), inputs, plain)
    total += dot(matrix(above, own_t, 0.0), left[0], plain)
    total += dot(matrix(below, other, 0.0), right[0], plain)
    mixed[...] = (total + own_first * inputs.astype(jnp.float32)).astype(jnp.bfloat16)
    total = dot(matrix(below, other_t, own), cotangent, plain)
    total += dot(matrix(below, own, 0.0), right[1], plain)
    total += dot(matrix(above, other_t, 0.0), left[1], plain)
    grad[...] = (total + other_first * cotangent.astype(jnp.float32)).astype(jnp.bfloat16)


def on_device(hidden, token_ids, embedding, filters, lengths, cotangent):
    shape = jax.ShapeDtypeStruct
    half = TAPS // 2
    symbols = pl.pallas_call(
        symbols_kernel,
        out_shape=shape((embedding.shape[0], ROWS), jnp.int32),
        in_specs=[],
        out_specs=VMEM,
        cost_estimate=cost(1 << 33, 1 << 24),
        compiler_params=ROOM,
    )()
    both = pl.pallas_call(
        inputs_kernel,
        out_shape=shape((2, ROWS, CHANS), jnp.bfloat16),
        in_specs=[VMEM] * 5,
        out_specs=VMEM,
        cost_estimate=cost(1, 1),
        compiler_params=ROOM,
    )(hidden, token_ids, embedding, cotangent, symbols)
    up = [(i, i + 1) for i in range(CTX_SIZE - 1)]
    left = lax.ppermute(both, CTX, up)
    right = lax.ppermute(both, CTX, [(j, i) for i, j in up])
    pair = (2, ROWS, ROWS)
    near = pl.pallas_call(
        near_kernel,
        out_shape=shape(pair, jnp.float32),
        in_specs=[VMEM],
        out_specs=VMEM,
        cost_estimate=cost(1, 1),
        compiler_params=ROOM,
    )(both)
    sums = pl.pallas_call(
        correlate_kernel,
        out_shape=shape((math.prod(SIZES[a] for a in FIRST), 4, half), jnp.float32),
        in_specs=[VMEM] * 3,
        out_specs=VMEM,
        cost_estimate=cost(1, 1),
        compiler_params=ROOM,
    )(both, right, near)
    sums = lax.all_to_all(sums, FIRST, 0, 0)
    block = shape((ROWS, CHANS), jnp.bfloat16)
    mixed, hidden_grad, factor = pl.pallas_call(
        outputs_kernel,
        out_shape=(block, block, shape((GROUPS, TAPS), jnp.float32)),
        in_specs=[VMEM] * 4 + [SMEM],
        out_specs=(VMEM,) * 3,
        cost_estimate=cost(1, 1),
        compiler_params=ROOM,
    )(both, left, right, filters, lengths)
    sums, factor = lax.optimization_barrier((sums, factor))
    sums = pl.pallas_call(
        sum_kernel,
        out_shape=shape((math.prod(SIZES[a] for a in SECOND), len(kept_places()), 4, half), jnp.float32),
        in_specs=[VMEM],
        out_specs=VMEM,
        cost_estimate=cost(1, 1),
        compiler_params=ROOM,
    )(sums)
    sums = lax.all_to_all(sums, SECOND, 0, 0)
    filter_grad = pl.pallas_call(
        finish_kernel,
        out_shape=shape((GROUPS, TAPS), jnp.float32),
        in_specs=[VMEM] * 2,
        out_specs=VMEM,
        cost_estimate=cost(1, 1),
        compiler_params=ROOM,
    )(sums, factor)
    return mixed, hidden_grad, filter_grad


def solution(mesh):
    names = tuple(name for name, _ in PARTS)
    fine = Mesh(mesh.devices.reshape([size for _, size in PARTS]), names)
    ctx, ch = names[:2], names[2:]
    placed = (P(ctx, ch), P(ctx), P(None, ch), P(), P(), P(ctx, ch))
    return jax.shard_map(
        on_device,
        mesh=fine,
        in_specs=placed,
        out_specs=(P(ctx, ch), P(ctx, ch), P()),
        check_vma=False,
    )
```

```python
import math

import jax
import jax.numpy as jnp
from jax import lax
from jax.experimental import pallas as pl
from jax.experimental.pallas import tpu as pltpu
from jax.sharding import Mesh, PartitionSpec as P

GW = 256
BT = 32
ROWS = 256
CHANS = 128
TAPS = 256
GROUPS = 16
PARTS = (("z", 8), ("x_lo", 2), ("x_hi", 2), ("y", 8), ("core", 2))
CTX = ("z", "x_lo")
FIRST = ('z', 'core')
SECOND = ('x_lo', 'x_hi', 'y')
SIZES = dict(PARTS)
ORDER1 = list(range(16))[::-1]
ORDER2 = list(range(32))[::-1]
CTX_SIZE = 16

VMEM = pl.BlockSpec(memory_space=pltpu.VMEM)
SMEM = pl.BlockSpec(memory_space=pltpu.SMEM)


def dot(a, b, contract):
    return lax.dot_general(a, b, (contract, ((), ())), preferred_element_type=jnp.float32)


def cost(flops, moved):
    return pl.CostEstimate(flops=flops, bytes_accessed=moved, transcendentals=0)


ROOM = pltpu.CompilerParams(vmem_limit_bytes=16 * 1024 * 1024)


def iota(shape, dim):
    return lax.broadcasted_iota(jnp.int32, shape, dim)


def symbols_kernel(symbols):
    symbols[...] = iota(symbols.shape, 0)


def inputs_kernel(hidden, ids, table, cotangent, symbols, both):
    ids_row = jnp.broadcast_to(ids[...].reshape(1, ROWS), symbols.shape)
    onehot = jnp.where(symbols[...] == ids_row, 1.0, 0.0)
    looked = dot(onehot, table[...].astype(jnp.float32), ((0,), (0,)))
    both[0] = (hidden[...].astype(jnp.float32) + looked).astype(jnp.bfloat16)
    both[1] = cotangent[...]


def lag_sums(product):
    half = ROWS // 2
    while half >= 8:
        product = product[:half] + pltpu.roll(product[half:], TAPS - half, 1)
        half //= 2
    row = iota(product.shape, 0)
    for step in (4, 2, 1):
        product = jnp.where((row & step) != 0, pltpu.roll(product, TAPS - step, 1), product)
    return jnp.sum(product, axis=0, keepdims=True)


LANE = ((1,), (1,))


def lag_here():
    shape = (ROWS, ROWS)
    return iota(shape, 1) >= iota(shape, 0)


def near_kernel(both, near):
    here = lag_here()
    for first, second in ((0, 1), (1, 0)):
        near[first] = jnp.where(here, dot(both[first], both[second], LANE), 0.0)


def correlate_kernel(both, right, near, out):
    here = lag_here()
    sums = []
    for first, second in ((0, 1), (1, 0)):
        far = dot(both[first], right[second], LANE)
        sums.append(lag_sums(jnp.where(here, near[first], far)))
    half = TAPS // 2
    pieces = [sums[0][:, :half], sums[0][:, half:], sums[1][:, :half], sums[1][:, half:]]
    row = iota((4, half), 0)
    packed = jnp.where(row < 2, jnp.where(row == 0, pieces[0], pieces[1]),
                       jnp.where(row == 2, pieces[2], pieces[3]))
    for peer in range(out.shape[0]):
        out[peer] = packed


def sources(axes, fixed):
    places = [0]
    for name in axes:
        size = SIZES[name]
        picks = [fixed[name]] if name in fixed else range(size)
        places = [place * size + pick for place in places for pick in picks]
    return places


def tree_sum(terms):
    while len(terms) > 1:
        terms = [sum(terms[i : i + 2][1:], terms[i]) for i in range(0, len(terms), 2)]
    return terms[0]


def kept_places():
    places = [{}]
    for name in FIRST:
        if name in ("x_hi", "y"):
            places = [dict(place, **{name: i}) for place in places for i in range(SIZES[name])]
    return places


def sum_kernel(parts, out):
    for kept, fixed in enumerate(kept_places()):
        total = tree_sum([parts[place] for place in map(ORDER1.index, sources(FIRST, fixed))])
        for peer in range(out.shape[0]):
            out[peer, kept] = total


def group_sum(parts, group):
    coords = {"x_hi": group // 8, "y": group % 8}
    kept = next(i for i, fixed in enumerate(kept_places()) if fixed.items() <= coords.items())
    return tree_sum([parts[place, kept] for place in map(ORDER2.index, sources(SECOND, coords))])


def finish_kernel(parts, factor, out):
    half = TAPS // 2
    total = [group_sum(parts, group) for group in range(GROUPS)]
    for group in range(GROUPS):
        own = total[group]
        other = total[GROUPS - 1 - group]
        out[group : group + 1, :half] = own[0:1] + other[2:3]
        out[group : group + 1, half:] = own[1:2] + other[3:4]
    scaled = factor[...]
    out[...] = jnp.where(scaled != 0.0, out[...] * scaled, 0.0)


def outputs_kernel(both, left, right, filters, lengths, mixed, grad, factor):
    taps_shape = (GROUPS, TAPS)
    group_row = iota(taps_shape, 0)
    tap_lane = iota(taps_shape, 1)
    reach = jnp.zeros(taps_shape, jnp.int32)
    for group in range(GROUPS):
        reach = jnp.where(group_row == group, lengths[group] * BT, reach)
    kept = tap_lane < reach
    scale = 1.0 / math.sqrt(ROWS * CTX_SIZE * GW)
    factor[...] = jnp.where(kept, scale, 0.0)
    taps = jnp.where(kept, filters[...].astype(jnp.float32), 0.0)
    mine = lax.axis_index("x_hi") * 8 + lax.axis_index("y")

    def circulant(index):
        row = jnp.sum(jnp.where(group_row == index, taps, 0.0), axis=0, keepdims=True)
        spread = pltpu.roll(jnp.broadcast_to(row, (ROWS, TAPS)), 0, 1, stride=1, stride_axis=0)
        return row[:, :1], spread, spread.T

    own_first, own, own_t = circulant(mine)
    other_first, other, other_t = circulant(GROUPS - 1 - mine)
    shape = (ROWS, ROWS)
    row, lane = iota(shape, 0), iota(shape, 1)
    below = row > lane
    above = row < lane

    def matrix(mask, yes, no):
        return jnp.where(mask, yes, no).astype(jnp.bfloat16)

    plain = ((1,), (0,))
    inputs, cotangent = both[0], both[1]
    total = dot(matrix(below, own_t, other), inputs, plain)
    total += dot(matrix(above, own_t, 0.0), left[0], plain)
    total += dot(matrix(below, other, 0.0), right[0], plain)
    mixed[...] = (total + own_first * inputs.astype(jnp.float32)).astype(jnp.bfloat16)
    total = dot(matrix(below, other_t, own), cotangent, plain)
    total += dot(matrix(below, own, 0.0), right[1], plain)
    total += dot(matrix(above, other_t, 0.0), left[1], plain)
    grad[...] = (total + other_first * cotangent.astype(jnp.float32)).astype(jnp.bfloat16)


def on_device(hidden, token_ids, embedding, filters, lengths, cotangent):
    shape = jax.ShapeDtypeStruct
    half = TAPS // 2
    symbols = pl.pallas_call(
        symbols_kernel,
        out_shape=shape((embedding.shape[0], ROWS), jnp.int32),
        in_specs=[],
        out_specs=VMEM,
        cost_estimate=cost(1 << 33, 1 << 24),
        compiler_params=ROOM,
    )()
    both = pl.pallas_call(
        inputs_kernel,
        out_shape=shape((2, ROWS, CHANS), jnp.bfloat16),
        in_specs=[VMEM] * 5,
        out_specs=VMEM,
        cost_estimate=cost(1, 1),
        compiler_params=ROOM,
    )(hidden, token_ids, embedding, cotangent, symbols)
    up = [(i, i + 1) for i in range(CTX_SIZE - 1)]
    left = lax.ppermute(both, CTX, up)
    right = lax.ppermute(both, CTX, [(j, i) for i, j in up])
    pair = (2, ROWS, ROWS)
    near = pl.pallas_call(
        near_kernel,
        out_shape=shape(pair, jnp.float32),
        in_specs=[VMEM],
        out_specs=VMEM,
        cost_estimate=cost(1, 1),
        compiler_params=ROOM,
    )(both)
    sums = pl.pallas_call(
        correlate_kernel,
        out_shape=shape((math.prod(SIZES[a] for a in FIRST), 4, half), jnp.float32),
        in_specs=[VMEM] * 3,
        out_specs=VMEM,
        cost_estimate=cost(1, 1),
        compiler_params=ROOM,
    )(both, right, near)
    sums = lax.all_to_all(sums, FIRST, 0, 0, axis_index_groups=[ORDER1])
    block = shape((ROWS, CHANS), jnp.bfloat16)
    mixed, hidden_grad, factor = pl.pallas_call(
        outputs_kernel,
        out_shape=(block, block, shape((GROUPS, TAPS), jnp.float32)),
        in_specs=[VMEM] * 4 + [SMEM],
        out_specs=(VMEM,) * 3,
        cost_estimate=cost(1, 1),
        compiler_params=ROOM,
    )(both, left, right, filters, lengths)
    sums, factor = lax.optimization_barrier((sums, factor))
    sums = pl.pallas_call(
        sum_kernel,
        out_shape=shape((math.prod(SIZES[a] for a in SECOND), len(kept_places()), 4, half), jnp.float32),
        in_specs=[VMEM],
        out_specs=VMEM,
        cost_estimate=cost(1, 1),
        compiler_params=ROOM,
    )(sums)
    sums = lax.all_to_all(sums, SECOND, 0, 0, axis_index_groups=[ORDER2])
    filter_grad = pl.pallas_call(
        finish_kernel,
        out_shape=shape((GROUPS, TAPS), jnp.float32),
        in_specs=[VMEM] * 2,
        out_specs=VMEM,
        cost_estimate=cost(1, 1),
        compiler_params=ROOM,
    )(sums, factor)
    return mixed, hidden_grad, filter_grad


def solution(mesh):
    names = tuple(name for name, _ in PARTS)
    fine = Mesh(mesh.devices.reshape([size for _, size in PARTS]), names)
    ctx, ch = names[:2], names[2:]
    placed = (P(ctx, ch), P(ctx), P(None, ch), P(), P(), P(ctx, ch))
    return jax.shard_map(
        on_device,
        mesh=fine,
        in_specs=placed,
        out_specs=(P(ctx, ch), P(ctx, ch), P()),
        check_vma=False,
    )
```

```python
import math

import jax
import jax.numpy as jnp
from jax import lax
from jax.experimental import pallas as pl
from jax.experimental.pallas import tpu as pltpu
from jax.sharding import Mesh, PartitionSpec as P

GW = 256
BT = 32
ROWS = 256
CHANS = 128
TAPS = 256
GROUPS = 16
PARTS = (("z", 8), ("x_lo", 2), ("x_hi", 2), ("y", 8), ("core", 2))
CTX = ("z", "x_lo")
FIRST = ('z', 'core')
SECOND = ('x_lo', 'x_hi', 'y')
SIZES = dict(PARTS)
ORDER1 = [(i + 12) % 16 for i in range(16)][::-1]
ORDER2 = [(i + 13) % 32 for i in range(32)][::-1]
CTX_SIZE = 16

VMEM = pl.BlockSpec(memory_space=pltpu.VMEM)
SMEM = pl.BlockSpec(memory_space=pltpu.SMEM)


def dot(a, b, contract):
    return lax.dot_general(a, b, (contract, ((), ())), preferred_element_type=jnp.float32)


def cost(flops, moved):
    return pl.CostEstimate(flops=flops, bytes_accessed=moved, transcendentals=0)


ROOM = pltpu.CompilerParams(vmem_limit_bytes=16 * 1024 * 1024)


def iota(shape, dim):
    return lax.broadcasted_iota(jnp.int32, shape, dim)


def symbols_kernel(symbols):
    symbols[...] = iota(symbols.shape, 0)


def inputs_kernel(hidden, ids, table, cotangent, symbols, both):
    ids_row = jnp.broadcast_to(ids[...].reshape(1, ROWS), symbols.shape)
    onehot = jnp.where(symbols[...] == ids_row, 1.0, 0.0)
    looked = dot(onehot, table[...].astype(jnp.float32), ((0,), (0,)))
    both[0] = (hidden[...].astype(jnp.float32) + looked).astype(jnp.bfloat16)
    both[1] = cotangent[...]


def lag_sums(product):
    half = ROWS // 2
    while half >= 8:
        product = product[:half] + pltpu.roll(product[half:], TAPS - half, 1)
        half //= 2
    row = iota(product.shape, 0)
    for step in (4, 2, 1):
        product = jnp.where((row & step) != 0, pltpu.roll(product, TAPS - step, 1), product)
    return jnp.sum(product, axis=0, keepdims=True)


LANE = ((1,), (1,))


def lag_here():
    shape = (ROWS, ROWS)
    return iota(shape, 1) >= iota(shape, 0)


def near_kernel(both, near):
    here = lag_here()
    for first, second in ((0, 1), (1, 0)):
        near[first] = jnp.where(here, dot(both[first], both[second], LANE), 0.0)


def correlate_kernel(both, right, near, out):
    here = lag_here()
    sums = []
    for first, second in ((0, 1), (1, 0)):
        far = dot(both[first], right[second], LANE)
        sums.append(lag_sums(jnp.where(here, near[first], far)))
    half = TAPS // 2
    pieces = [sums[0][:, :half], sums[0][:, half:], sums[1][:, :half], sums[1][:, half:]]
    row = iota((4, half), 0)
    packed = jnp.where(row < 2, jnp.where(row == 0, pieces[0], pieces[1]),
                       jnp.where(row == 2, pieces[2], pieces[3]))
    for peer in range(out.shape[0]):
        out[peer] = packed


def sources(axes, fixed):
    places = [0]
    for name in axes:
        size = SIZES[name]
        picks = [fixed[name]] if name in fixed else range(size)
        places = [place * size + pick for place in places for pick in picks]
    return places


def tree_sum(terms):
    while len(terms) > 1:
        terms = [sum(terms[i : i + 2][1:], terms[i]) for i in range(0, len(terms), 2)]
    return terms[0]


def kept_places():
    places = [{}]
    for name in FIRST:
        if name in ("x_hi", "y"):
            places = [dict(place, **{name: i}) for place in places for i in range(SIZES[name])]
    return places


def sum_kernel(parts, out):
    for kept, fixed in enumerate(kept_places()):
        total = tree_sum([parts[place] for place in map(ORDER1.index, sources(FIRST, fixed))])
        for peer in range(out.shape[0]):
            out[peer, kept] = total


def group_sum(parts, group):
    coords = {"x_hi": group // 8, "y": group % 8}
    kept = next(i for i, fixed in enumerate(kept_places()) if fixed.items() <= coords.items())
    return tree_sum([parts[place, kept] for place in map(ORDER2.index, sources(SECOND, coords))])


def finish_kernel(parts, factor, out):
    half = TAPS // 2
    total = [group_sum(parts, group) for group in range(GROUPS)]
    for group in range(GROUPS):
        own = total[group]
        other = total[GROUPS - 1 - group]
        out[group : group + 1, :half] = own[0:1] + other[2:3]
        out[group : group + 1, half:] = own[1:2] + other[3:4]
    scaled = factor[...]
    out[...] = jnp.where(scaled != 0.0, out[...] * scaled, 0.0)


def outputs_kernel(both, left, right, filters, lengths, mixed, grad, factor):
    taps_shape = (GROUPS, TAPS)
    group_row = iota(taps_shape, 0)
    tap_lane = iota(taps_shape, 1)
    reach = jnp.zeros(taps_shape, jnp.int32)
    for group in range(GROUPS):
        reach = jnp.where(group_row == group, lengths[group] * BT, reach)
    kept = tap_lane < reach
    scale = 1.0 / math.sqrt(ROWS * CTX_SIZE * GW)
    factor[...] = jnp.where(kept, scale, 0.0)
    taps = jnp.where(kept, filters[...].astype(jnp.float32), 0.0)
    mine = lax.axis_index("x_hi") * 8 + lax.axis_index("y")

    def circulant(index):
        row = jnp.sum(jnp.where(group_row == index, taps, 0.0), axis=0, keepdims=True)
        spread = pltpu.roll(jnp.broadcast_to(row, (ROWS, TAPS)), 0, 1, stride=1, stride_axis=0)
        return row[:, :1], spread, spread.T

    own_first, own, own_t = circulant(mine)
    other_first, other, other_t = circulant(GROUPS - 1 - mine)
    shape = (ROWS, ROWS)
    row, lane = iota(shape, 0), iota(shape, 1)
    below = row > lane
    above = row < lane

    def matrix(mask, yes, no):
        return jnp.where(mask, yes, no).astype(jnp.bfloat16)

    plain = ((1,), (0,))
    inputs, cotangent = both[0], both[1]
    total = dot(matrix(below, own_t, other), inputs, plain)
    total += dot(matrix(above, own_t, 0.0), left[0], plain)
    total += dot(matrix(below, other, 0.0), right[0], plain)
    mixed[...] = (total + own_first * inputs.astype(jnp.float32)).astype(jnp.bfloat16)
    total = dot(matrix(below, other_t, own), cotangent, plain)
    total += dot(matrix(below, own, 0.0), right[1], plain)
    total += dot(matrix(above, other_t, 0.0), left[1], plain)
    grad[...] = (total + other_first * cotangent.astype(jnp.float32)).astype(jnp.bfloat16)


def on_device(hidden, token_ids, embedding, filters, lengths, cotangent):
    shape = jax.ShapeDtypeStruct
    half = TAPS // 2
    symbols = pl.pallas_call(
        symbols_kernel,
        out_shape=shape((embedding.shape[0], ROWS), jnp.int32),
        in_specs=[],
        out_specs=VMEM,
        cost_estimate=cost(1 << 33, 1 << 24),
        compiler_params=ROOM,
    )()
    both = pl.pallas_call(
        inputs_kernel,
        out_shape=shape((2, ROWS, CHANS), jnp.bfloat16),
        in_specs=[VMEM] * 5,
        out_specs=VMEM,
        cost_estimate=cost(1, 1),
        compiler_params=ROOM,
    )(hidden, token_ids, embedding, cotangent, symbols)
    up = [(i, i + 1) for i in range(CTX_SIZE - 1)]
    left = lax.ppermute(both, CTX, up)
    right = lax.ppermute(both, CTX, [(j, i) for i, j in up])
    pair = (2, ROWS, ROWS)
    near = pl.pallas_call(
        near_kernel,
        out_shape=shape(pair, jnp.float32),
        in_specs=[VMEM],
        out_specs=VMEM,
        cost_estimate=cost(1, 1),
        compiler_params=ROOM,
    )(both)
    sums = pl.pallas_call(
        correlate_kernel,
        out_shape=shape((math.prod(SIZES[a] for a in FIRST), 4, half), jnp.float32),
        in_specs=[VMEM] * 3,
        out_specs=VMEM,
        cost_estimate=cost(1, 1),
        compiler_params=ROOM,
    )(both, right, near)
    sums = lax.all_to_all(sums, FIRST, 0, 0, axis_index_groups=[ORDER1])
    block = shape((ROWS, CHANS), jnp.bfloat16)
    mixed, hidden_grad, factor = pl.pallas_call(
        outputs_kernel,
        out_shape=(block, block, shape((GROUPS, TAPS), jnp.float32)),
        in_specs=[VMEM] * 4 + [SMEM],
        out_specs=(VMEM,) * 3,
        cost_estimate=cost(1, 1),
        compiler_params=ROOM,
    )(both, left, right, filters, lengths)
    sums, factor = lax.optimization_barrier((sums, factor))
    sums = pl.pallas_call(
        sum_kernel,
        out_shape=shape((math.prod(SIZES[a] for a in SECOND), len(kept_places()), 4, half), jnp.float32),
        in_specs=[VMEM],
        out_specs=VMEM,
        cost_estimate=cost(1, 1),
        compiler_params=ROOM,
    )(sums)
    sums = lax.all_to_all(sums, SECOND, 0, 0, axis_index_groups=[ORDER2])
    filter_grad = pl.pallas_call(
        finish_kernel,
        out_shape=shape((GROUPS, TAPS), jnp.float32),
        in_specs=[VMEM] * 2,
        out_specs=VMEM,
        cost_estimate=cost(1, 1),
        compiler_params=ROOM,
    )(sums, factor)
    return mixed, hidden_grad, filter_grad


def solution(mesh):
    names = tuple(name for name, _ in PARTS)
    fine = Mesh(mesh.devices.reshape([size for _, size in PARTS]), names)
    ctx, ch = names[:2], names[2:]
    placed = (P(ctx, ch), P(ctx), P(None, ch), P(), P(), P(ctx, ch))
    return jax.shard_map(
        on_device,
        mesh=fine,
        in_specs=placed,
        out_specs=(P(ctx, ch), P(ctx, ch), P()),
        check_vma=False,
    )
```

```python
import math

import jax
import jax.numpy as jnp
from jax import lax
from jax.experimental import pallas as pl
from jax.experimental.pallas import tpu as pltpu
from jax.sharding import Mesh, PartitionSpec as P

GW = 256
BT = 32
ROWS = 256
CHANS = 128
TAPS = 256
GROUPS = 16
PARTS = (("z", 8), ("x_lo", 2), ("x_hi", 2), ("y", 8), ("core", 2))
CTX = ("z", "x_lo")
FIRST = ('z', 'core')
SECOND = ('x_lo', 'x_hi', 'y')
SIZES = dict(PARTS)
ORDER1 = [(i + 12) % 16 for i in range(16)][::-1]
ORDER2 = [(i + 13) % 32 for i in range(32)][::-1]
CTX_SIZE = 16

VMEM = pl.BlockSpec(memory_space=pltpu.VMEM)
SMEM = pl.BlockSpec(memory_space=pltpu.SMEM)


def dot(a, b, contract):
    return lax.dot_general(a, b, (contract, ((), ())), preferred_element_type=jnp.float32)


def cost(flops, moved):
    return pl.CostEstimate(flops=flops, bytes_accessed=moved, transcendentals=0)


ROOM = pltpu.CompilerParams(vmem_limit_bytes=16 * 1024 * 1024)


def iota(shape, dim):
    return lax.broadcasted_iota(jnp.int32, shape, dim)


def symbols_kernel(symbols):
    symbols[...] = iota(symbols.shape, 0)


def inputs_kernel(hidden, ids, table, cotangent, symbols, both):
    ids_row = jnp.broadcast_to(ids[...].reshape(1, ROWS), symbols.shape)
    onehot = jnp.where(symbols[...] == ids_row, 1.0, 0.0)
    looked = dot(onehot, table[...].astype(jnp.float32), ((0,), (0,)))
    both[0] = (hidden[...].astype(jnp.float32) + looked).astype(jnp.bfloat16)
    both[1] = cotangent[...]


def lag_sums(product):
    for rows, parts in ((64, 4), (16, 4), (8, 2)):
        pieces = [product[:rows]]
        for part in range(1, parts):
            piece = product[part * rows : (part + 1) * rows]
            pieces.append(pltpu.roll(piece, TAPS - part * rows, 1))
        product = tree_sum(pieces)
    row = iota(product.shape, 0)
    rolled = [pltpu.roll(product, TAPS - step, 1) for step in range(1, 8)]
    for step, piece in enumerate(rolled, 1):
        product = jnp.where(row == step, piece, product)
    return jnp.sum(product, axis=0, keepdims=True)


LANE = ((1,), (1,))


def lag_here():
    shape = (ROWS, ROWS)
    return iota(shape, 1) >= iota(shape, 0)


def near_kernel(both, near):
    here = lag_here()
    for first, second in ((0, 1), (1, 0)):
        near[first] = jnp.where(here, dot(both[first], both[second], LANE), 0.0)


def correlate_kernel(both, right, near, out):
    here = lag_here()
    sums = []
    for first, second in ((0, 1), (1, 0)):
        far = dot(both[first], right[second], LANE)
        sums.append(lag_sums(jnp.where(here, near[first], far)))
    half = TAPS // 2
    pieces = [sums[0][:, :half], sums[0][:, half:], sums[1][:, :half], sums[1][:, half:]]
    row = iota((4, half), 0)
    packed = jnp.where(row < 2, jnp.where(row == 0, pieces[0], pieces[1]),
                       jnp.where(row == 2, pieces[2], pieces[3]))
    for peer in range(out.shape[0]):
        out[peer] = packed


def sources(axes, fixed):
    places = [0]
    for name in axes:
        size = SIZES[name]
        picks = [fixed[name]] if name in fixed else range(size)
        places = [place * size + pick for place in places for pick in picks]
    return places


def tree_sum(terms):
    while len(terms) > 1:
        terms = [sum(terms[i : i + 2][1:], terms[i]) for i in range(0, len(terms), 2)]
    return terms[0]


def kept_places():
    places = [{}]
    for name in FIRST:
        if name in ("x_hi", "y"):
            places = [dict(place, **{name: i}) for place in places for i in range(SIZES[name])]
    return places


def sum_kernel(parts, out):
    for kept, fixed in enumerate(kept_places()):
        total = tree_sum([parts[place] for place in map(ORDER1.index, sources(FIRST, fixed))])
        for peer in range(out.shape[0]):
            out[peer, kept] = total


def group_sum(parts, group):
    coords = {"x_hi": group // 8, "y": group % 8}
    kept = next(i for i, fixed in enumerate(kept_places()) if fixed.items() <= coords.items())
    return tree_sum([parts[place, kept] for place in map(ORDER2.index, sources(SECOND, coords))])


def finish_kernel(parts, factor, out):
    half = TAPS // 2
    total = [group_sum(parts, group) for group in range(GROUPS)]
    for group in range(GROUPS):
        own = total[group]
        other = total[GROUPS - 1 - group]
        out[group : group + 1, :half] = own[0:1] + other[2:3]
        out[group : group + 1, half:] = own[1:2] + other[3:4]
    scaled = factor[...]
    out[...] = jnp.where(scaled != 0.0, out[...] * scaled, 0.0)


def outputs_kernel(both, left, right, filters, lengths, mixed, grad, factor):
    taps_shape = (GROUPS, TAPS)
    group_row = iota(taps_shape, 0)
    tap_lane = iota(taps_shape, 1)
    reach = jnp.zeros(taps_shape, jnp.int32)
    for group in range(GROUPS):
        reach = jnp.where(group_row == group, lengths[group] * BT, reach)
    kept = tap_lane < reach
    scale = 1.0 / math.sqrt(ROWS * CTX_SIZE * GW)
    factor[...] = jnp.where(kept, scale, 0.0)
    taps = jnp.where(kept, filters[...].astype(jnp.float32), 0.0)
    mine = lax.axis_index("x_hi") * 8 + lax.axis_index("y")

    def circulant(index):
        row = jnp.sum(jnp.where(group_row == index, taps, 0.0), axis=0, keepdims=True)
        spread = pltpu.roll(jnp.broadcast_to(row, (ROWS, TAPS)), 0, 1, stride=1, stride_axis=0)
        return row[:, :1], spread, spread.T

    own_first, own, own_t = circulant(mine)
    other_first, other, other_t = circulant(GROUPS - 1 - mine)
    shape = (ROWS, ROWS)
    row, lane = iota(shape, 0), iota(shape, 1)
    below = row > lane
    above = row < lane

    def matrix(mask, yes, no):
        return jnp.where(mask, yes, no).astype(jnp.bfloat16)

    plain = ((1,), (0,))
    inputs, cotangent = both[0], both[1]
    total = dot(matrix(below, own_t, other), inputs, plain)
    total += dot(matrix(above, own_t, 0.0), left[0], plain)
    total += dot(matrix(below, other, 0.0), right[0], plain)
    mixed[...] = (total + own_first * inputs.astype(jnp.float32)).astype(jnp.bfloat16)
    total = dot(matrix(below, other_t, own), cotangent, plain)
    total += dot(matrix(below, own, 0.0), right[1], plain)
    total += dot(matrix(above, other_t, 0.0), left[1], plain)
    grad[...] = (total + other_first * cotangent.astype(jnp.float32)).astype(jnp.bfloat16)


def on_device(hidden, token_ids, embedding, filters, lengths, cotangent):
    shape = jax.ShapeDtypeStruct
    half = TAPS // 2
    symbols = pl.pallas_call(
        symbols_kernel,
        out_shape=shape((embedding.shape[0], ROWS), jnp.int32),
        in_specs=[],
        out_specs=VMEM,
        cost_estimate=cost(1 << 33, 1 << 24),
        compiler_params=ROOM,
    )()
    both = pl.pallas_call(
        inputs_kernel,
        out_shape=shape((2, ROWS, CHANS), jnp.bfloat16),
        in_specs=[VMEM] * 5,
        out_specs=VMEM,
        cost_estimate=cost(1, 1),
        compiler_params=ROOM,
    )(hidden, token_ids, embedding, cotangent, symbols)
    up = [(i, i + 1) for i in range(CTX_SIZE - 1)]
    left = lax.ppermute(both, CTX, up)
    right = lax.ppermute(both, CTX, [(j, i) for i, j in up])
    pair = (2, ROWS, ROWS)
    near = pl.pallas_call(
        near_kernel,
        out_shape=shape(pair, jnp.float32),
        in_specs=[VMEM],
        out_specs=VMEM,
        cost_estimate=cost(1, 1),
        compiler_params=ROOM,
    )(both)
    sums = pl.pallas_call(
        correlate_kernel,
        out_shape=shape((math.prod(SIZES[a] for a in FIRST), 4, half), jnp.float32),
        in_specs=[VMEM] * 3,
        out_specs=VMEM,
        cost_estimate=cost(1, 1),
        compiler_params=ROOM,
    )(both, right, near)
    sums = lax.all_to_all(sums, FIRST, 0, 0, axis_index_groups=[ORDER1])
    block = shape((ROWS, CHANS), jnp.bfloat16)
    mixed, hidden_grad, factor = pl.pallas_call(
        outputs_kernel,
        out_shape=(block, block, shape((GROUPS, TAPS), jnp.float32)),
        in_specs=[VMEM] * 4 + [SMEM],
        out_specs=(VMEM,) * 3,
        cost_estimate=cost(1, 1),
        compiler_params=ROOM,
    )(both, left, right, filters, lengths)
    sums, factor = lax.optimization_barrier((sums, factor))
    sums = pl.pallas_call(
        sum_kernel,
        out_shape=shape((math.prod(SIZES[a] for a in SECOND), len(kept_places()), 4, half), jnp.float32),
        in_specs=[VMEM],
        out_specs=VMEM,
        cost_estimate=cost(1, 1),
        compiler_params=ROOM,
    )(sums)
    sums = lax.all_to_all(sums, SECOND, 0, 0, axis_index_groups=[ORDER2])
    filter_grad = pl.pallas_call(
        finish_kernel,
        out_shape=shape((GROUPS, TAPS), jnp.float32),
        in_specs=[VMEM] * 2,
        out_specs=VMEM,
        cost_estimate=cost(1, 1),
        compiler_params=ROOM,
    )(sums, factor)
    return mixed, hidden_grad, filter_grad


def solution(mesh):
    names = tuple(name for name, _ in PARTS)
    fine = Mesh(mesh.devices.reshape([size for _, size in PARTS]), names)
    ctx, ch = names[:2], names[2:]
    placed = (P(ctx, ch), P(ctx), P(None, ch), P(), P(), P(ctx, ch))
    return jax.shard_map(
        on_device,
        mesh=fine,
        in_specs=placed,
        out_specs=(P(ctx, ch), P(ctx, ch), P()),
        check_vma=False,
    )
```

```python
import math

import jax
import jax.numpy as jnp
from jax import lax
from jax.experimental import pallas as pl
from jax.experimental.pallas import tpu as pltpu
from jax.sharding import Mesh, PartitionSpec as P

GW = 256
BT = 32
ROWS = 256
CHANS = 128
TAPS = 256
GROUPS = 16
PARTS = (("z", 8), ("x_lo", 2), ("x_hi", 2), ("y", 8), ("core", 2))
CTX = ("z", "x_lo")
FIRST = ('z', 'core')
SECOND = ('x_lo', 'x_hi', 'y')
SIZES = dict(PARTS)
ORDER1 = [(i + 12) % 16 for i in range(16)][::-1]
ORDER2 = [(i + 13) % 32 for i in range(32)][::-1]
CTX_SIZE = 16

VMEM = pl.BlockSpec(memory_space=pltpu.VMEM)
SMEM = pl.BlockSpec(memory_space=pltpu.SMEM)


def dot(a, b, contract):
    return lax.dot_general(a, b, (contract, ((), ())), preferred_element_type=jnp.float32)


def cost(flops, moved):
    return pl.CostEstimate(flops=flops, bytes_accessed=moved, transcendentals=0)


ROOM = pltpu.CompilerParams(vmem_limit_bytes=16 * 1024 * 1024)


def iota(shape, dim):
    return lax.broadcasted_iota(jnp.int32, shape, dim)


def symbols_kernel(symbols):
    symbols[...] = iota(symbols.shape, 0)


def inputs_kernel(hidden, ids, table, cotangent, symbols, both):
    ids_row = jnp.broadcast_to(ids[...].reshape(1, ROWS), symbols.shape)
    onehot = jnp.where(symbols[...] == ids_row, 1.0, 0.0)
    looked = dot(onehot, table[...].astype(jnp.float32), ((0,), (0,)))
    both[0] = (hidden[...].astype(jnp.float32) + looked).astype(jnp.bfloat16)
    both[1] = cotangent[...]


def fold_rows(product):
    for rows, parts in ((64, 4), (16, 4), (8, 2)):
        pieces = [product[:rows]]
        for part in range(1, parts):
            piece = product[part * rows : (part + 1) * rows]
            pieces.append(pltpu.roll(piece, TAPS - part * rows, 1))
        product = tree_sum(pieces)
    return product


def lag_sums(product):
    row = iota(product.shape, 0)
    rolled = [pltpu.roll(product, TAPS - step, 1) for step in range(1, 8)]
    for step, piece in enumerate(rolled, 1):
        product = jnp.where(row == step, piece, product)
    return jnp.sum(product, axis=0, keepdims=True)


LANE = ((1,), (1,))


def lag_here():
    shape = (ROWS, ROWS)
    return iota(shape, 1) >= iota(shape, 0)


def near_kernel(both, near):
    here = lag_here()
    for first, second in ((0, 1), (1, 0)):
        near[first] = fold_rows(jnp.where(here, dot(both[first], both[second], LANE), 0.0))


def correlate_kernel(both, right, near, out):
    here = lag_here()
    sums = []
    for first, second in ((0, 1), (1, 0)):
        far = dot(both[first], right[second], LANE)
        sums.append(lag_sums(fold_rows(jnp.where(here, 0.0, far)) + near[first]))
    half = TAPS // 2
    pieces = [sums[0][:, :half], sums[0][:, half:], sums[1][:, :half], sums[1][:, half:]]
    row = iota((4, half), 0)
    packed = jnp.where(row < 2, jnp.where(row == 0, pieces[0], pieces[1]),
                       jnp.where(row == 2, pieces[2], pieces[3]))
    for peer in range(out.shape[0]):
        out[peer] = packed


def sources(axes, fixed):
    places = [0]
    for name in axes:
        size = SIZES[name]
        picks = [fixed[name]] if name in fixed else range(size)
        places = [place * size + pick for place in places for pick in picks]
    return places


def tree_sum(terms):
    while len(terms) > 1:
        terms = [sum(terms[i : i + 2][1:], terms[i]) for i in range(0, len(terms), 2)]
    return terms[0]


def kept_places():
    places = [{}]
    for name in FIRST:
        if name in ("x_hi", "y"):
            places = [dict(place, **{name: i}) for place in places for i in range(SIZES[name])]
    return places


def sum_kernel(parts, out):
    for kept, fixed in enumerate(kept_places()):
        total = tree_sum([parts[place] for place in map(ORDER1.index, sources(FIRST, fixed))])
        for peer in range(out.shape[0]):
            out[peer, kept] = total


def group_sum(parts, group):
    coords = {"x_hi": group // 8, "y": group % 8}
    kept = next(i for i, fixed in enumerate(kept_places()) if fixed.items() <= coords.items())
    return tree_sum([parts[place, kept] for place in map(ORDER2.index, sources(SECOND, coords))])


def finish_kernel(parts, factor, out):
    half = TAPS // 2
    total = [group_sum(parts, group) for group in range(GROUPS)]
    for group in range(GROUPS):
        own = total[group]
        other = total[GROUPS - 1 - group]
        out[group : group + 1, :half] = own[0:1] + other[2:3]
        out[group : group + 1, half:] = own[1:2] + other[3:4]
    scaled = factor[...]
    out[...] = jnp.where(scaled != 0.0, out[...] * scaled, 0.0)


def outputs_kernel(both, left, right, filters, lengths, mixed, grad, factor):
    taps_shape = (GROUPS, TAPS)
    group_row = iota(taps_shape, 0)
    tap_lane = iota(taps_shape, 1)
    reach = jnp.zeros(taps_shape, jnp.int32)
    for group in range(GROUPS):
        reach = jnp.where(group_row == group, lengths[group] * BT, reach)
    kept = tap_lane < reach
    scale = 1.0 / math.sqrt(ROWS * CTX_SIZE * GW)
    factor[...] = jnp.where(kept, scale, 0.0)
    taps = jnp.where(kept, filters[...].astype(jnp.float32), 0.0)
    mine = lax.axis_index("x_hi") * 8 + lax.axis_index("y")

    def circulant(index):
        row = jnp.sum(jnp.where(group_row == index, taps, 0.0), axis=0, keepdims=True)
        spread = pltpu.roll(jnp.broadcast_to(row, (ROWS, TAPS)), 0, 1, stride=1, stride_axis=0)
        return row[:, :1], spread, spread.T

    own_first, own, own_t = circulant(mine)
    other_first, other, other_t = circulant(GROUPS - 1 - mine)
    shape = (ROWS, ROWS)
    row, lane = iota(shape, 0), iota(shape, 1)
    below = row > lane
    above = row < lane

    def matrix(mask, yes, no):
        return jnp.where(mask, yes, no).astype(jnp.bfloat16)

    plain = ((1,), (0,))
    inputs, cotangent = both[0], both[1]
    total = dot(matrix(below, own_t, other), inputs, plain)
    total += dot(matrix(above, own_t, 0.0), left[0], plain)
    total += dot(matrix(below, other, 0.0), right[0], plain)
    mixed[...] = (total + own_first * inputs.astype(jnp.float32)).astype(jnp.bfloat16)
    total = dot(matrix(below, other_t, own), cotangent, plain)
    total += dot(matrix(below, own, 0.0), right[1], plain)
    total += dot(matrix(above, other_t, 0.0), left[1], plain)
    grad[...] = (total + other_first * cotangent.astype(jnp.float32)).astype(jnp.bfloat16)


def on_device(hidden, token_ids, embedding, filters, lengths, cotangent):
    shape = jax.ShapeDtypeStruct
    half = TAPS // 2
    symbols = pl.pallas_call(
        symbols_kernel,
        out_shape=shape((embedding.shape[0], ROWS), jnp.int32),
        in_specs=[],
        out_specs=VMEM,
        cost_estimate=cost(1 << 33, 1 << 24),
        compiler_params=ROOM,
    )()
    both = pl.pallas_call(
        inputs_kernel,
        out_shape=shape((2, ROWS, CHANS), jnp.bfloat16),
        in_specs=[VMEM] * 5,
        out_specs=VMEM,
        cost_estimate=cost(1, 1),
        compiler_params=ROOM,
    )(hidden, token_ids, embedding, cotangent, symbols)
    up = [(i, i + 1) for i in range(CTX_SIZE - 1)]
    left = lax.ppermute(both, CTX, up)
    right = lax.ppermute(both, CTX, [(j, i) for i, j in up])
    pair = (2, 8, ROWS)
    near = pl.pallas_call(
        near_kernel,
        out_shape=shape(pair, jnp.float32),
        in_specs=[VMEM],
        out_specs=VMEM,
        cost_estimate=cost(1, 1),
        compiler_params=ROOM,
    )(both)
    sums = pl.pallas_call(
        correlate_kernel,
        out_shape=shape((math.prod(SIZES[a] for a in FIRST), 4, half), jnp.float32),
        in_specs=[VMEM] * 3,
        out_specs=VMEM,
        cost_estimate=cost(1, 1),
        compiler_params=ROOM,
    )(both, right, near)
    sums = lax.all_to_all(sums, FIRST, 0, 0, axis_index_groups=[ORDER1])
    block = shape((ROWS, CHANS), jnp.bfloat16)
    mixed, hidden_grad, factor = pl.pallas_call(
        outputs_kernel,
        out_shape=(block, block, shape((GROUPS, TAPS), jnp.float32)),
        in_specs=[VMEM] * 4 + [SMEM],
        out_specs=(VMEM,) * 3,
        cost_estimate=cost(1, 1),
        compiler_params=ROOM,
    )(both, left, right, filters, lengths)
    sums, factor = lax.optimization_barrier((sums, factor))
    sums = pl.pallas_call(
        sum_kernel,
        out_shape=shape((math.prod(SIZES[a] for a in SECOND), len(kept_places()), 4, half), jnp.float32),
        in_specs=[VMEM],
        out_specs=VMEM,
        cost_estimate=cost(1, 1),
        compiler_params=ROOM,
    )(sums)
    sums = lax.all_to_all(sums, SECOND, 0, 0, axis_index_groups=[ORDER2])
    filter_grad = pl.pallas_call(
        finish_kernel,
        out_shape=shape((GROUPS, TAPS), jnp.float32),
        in_specs=[VMEM] * 2,
        out_specs=VMEM,
        cost_estimate=cost(1, 1),
        compiler_params=ROOM,
    )(sums, factor)
    return mixed, hidden_grad, filter_grad


def solution(mesh):
    names = tuple(name for name, _ in PARTS)
    fine = Mesh(mesh.devices.reshape([size for _, size in PARTS]), names)
    ctx, ch = names[:2], names[2:]
    placed = (P(ctx, ch), P(ctx), P(None, ch), P(), P(), P(ctx, ch))
    return jax.shard_map(
        on_device,
        mesh=fine,
        in_specs=placed,
        out_specs=(P(ctx, ch), P(ctx, ch), P()),
        check_vma=False,
    )
```

```python
import math

import jax
import jax.numpy as jnp
from jax import lax
from jax.experimental import pallas as pl
from jax.experimental.pallas import tpu as pltpu
from jax.sharding import Mesh, PartitionSpec as P

GW = 256
BT = 32
ROWS = 256
CHANS = 128
TAPS = 256
GROUPS = 16
PARTS = (("z", 8), ("x_lo", 2), ("x_hi", 2), ("y", 8), ("core", 2))
CTX = ("z", "x_lo")
FIRST = ('z', 'core')
SECOND = ('x_lo', 'x_hi', 'y')
SIZES = dict(PARTS)
ORDER1 = [(i + 10) % 16 for i in range(16)][::-1]
ORDER2 = [(i + 13) % 32 for i in range(32)][::-1]
CTX_SIZE = 16

VMEM = pl.BlockSpec(memory_space=pltpu.VMEM)
SMEM = pl.BlockSpec(memory_space=pltpu.SMEM)


def dot(a, b, contract):
    return lax.dot_general(a, b, (contract, ((), ())), preferred_element_type=jnp.float32)


def cost(flops, moved):
    return pl.CostEstimate(flops=flops, bytes_accessed=moved, transcendentals=0)


ROOM = pltpu.CompilerParams(vmem_limit_bytes=16 * 1024 * 1024)


def iota(shape, dim):
    return lax.broadcasted_iota(jnp.int32, shape, dim)


def symbols_kernel(symbols):
    symbols[...] = iota(symbols.shape, 0)


def inputs_kernel(hidden, ids, table, cotangent, symbols, both):
    ids_row = jnp.broadcast_to(ids[...].reshape(1, ROWS), symbols.shape)
    onehot = jnp.where(symbols[...] == ids_row, 1.0, 0.0)
    looked = dot(onehot, table[...].astype(jnp.float32), ((0,), (0,)))
    both[0] = (hidden[...].astype(jnp.float32) + looked).astype(jnp.bfloat16)
    both[1] = cotangent[...]


def fold_rows(product):
    for rows, parts in ((64, 4), (16, 4), (8, 2)):
        pieces = [product[:rows]]
        for part in range(1, parts):
            piece = product[part * rows : (part + 1) * rows]
            pieces.append(pltpu.roll(piece, TAPS - part * rows, 1))
        product = tree_sum(pieces)
    return product


def lag_sums(product):
    row = iota(product.shape, 0)
    rolled = [pltpu.roll(product, TAPS - step, 1) for step in range(1, 8)]
    for step, piece in enumerate(rolled, 1):
        product = jnp.where(row == step, piece, product)
    return jnp.sum(product, axis=0, keepdims=True)


LANE = ((1,), (1,))


def lag_here():
    shape = (ROWS, ROWS)
    return iota(shape, 1) >= iota(shape, 0)


def near_kernel(both, near):
    here = lag_here()
    for first, second in ((0, 1), (1, 0)):
        near[first] = fold_rows(jnp.where(here, dot(both[first], both[second], LANE), 0.0))


def correlate_kernel(both, right, near, out):
    here = lag_here()
    sums = []
    for first, second in ((0, 1), (1, 0)):
        far = dot(both[first], right[second], LANE)
        sums.append(lag_sums(fold_rows(jnp.where(here, 0.0, far)) + near[first]))
    half = TAPS // 2
    pieces = [sums[0][:, :half], sums[0][:, half:], sums[1][:, :half], sums[1][:, half:]]
    row = iota((4, half), 0)
    packed = jnp.where(row < 2, jnp.where(row == 0, pieces[0], pieces[1]),
                       jnp.where(row == 2, pieces[2], pieces[3]))
    for peer in range(out.shape[0]):
        out[peer] = packed


def sources(axes, fixed):
    places = [0]
    for name in axes:
        size = SIZES[name]
        picks = [fixed[name]] if name in fixed else range(size)
        places = [place * size + pick for place in places for pick in picks]
    return places


def tree_sum(terms):
    while len(terms) > 1:
        terms = [sum(terms[i : i + 2][1:], terms[i]) for i in range(0, len(terms), 2)]
    return terms[0]


def kept_places():
    places = [{}]
    for name in FIRST:
        if name in ("x_hi", "y"):
            places = [dict(place, **{name: i}) for place in places for i in range(SIZES[name])]
    return places


def sum_kernel(parts, out):
    for kept, fixed in enumerate(kept_places()):
        total = tree_sum([parts[place] for place in map(ORDER1.index, sources(FIRST, fixed))])
        for peer in range(out.shape[0]):
            out[peer, kept] = total


def group_sum(parts, group):
    coords = {"x_hi": group // 8, "y": group % 8}
    kept = next(i for i, fixed in enumerate(kept_places()) if fixed.items() <= coords.items())
    return tree_sum([parts[place, kept] for place in map(ORDER2.index, sources(SECOND, coords))])


def finish_kernel(parts, factor, out):
    half = TAPS // 2
    total = [group_sum(parts, group) for group in range(GROUPS)]
    for group in range(GROUPS):
        own = total[group]
        other = total[GROUPS - 1 - group]
        out[group : group + 1, :half] = own[0:1] + other[2:3]
        out[group : group + 1, half:] = own[1:2] + other[3:4]
    scaled = factor[...]
    out[...] = jnp.where(scaled != 0.0, out[...] * scaled, 0.0)


def outputs_kernel(both, left, right, filters, lengths, mixed, grad, factor):
    taps_shape = (GROUPS, TAPS)
    group_row = iota(taps_shape, 0)
    tap_lane = iota(taps_shape, 1)
    reach = jnp.zeros(taps_shape, jnp.int32)
    for group in range(GROUPS):
        reach = jnp.where(group_row == group, lengths[group] * BT, reach)
    kept = tap_lane < reach
    scale = 1.0 / math.sqrt(ROWS * CTX_SIZE * GW)
    factor[...] = jnp.where(kept, scale, 0.0)
    taps = jnp.where(kept, filters[...].astype(jnp.float32), 0.0)
    mine = lax.axis_index("x_hi") * 8 + lax.axis_index("y")

    def circulant(index):
        row = jnp.sum(jnp.where(group_row == index, taps, 0.0), axis=0, keepdims=True)
        spread = pltpu.roll(jnp.broadcast_to(row, (ROWS, TAPS)), 0, 1, stride=1, stride_axis=0)
        return row[:, :1], spread, spread.T

    own_first, own, own_t = circulant(mine)
    other_first, other, other_t = circulant(GROUPS - 1 - mine)
    shape = (ROWS, ROWS)
    row, lane = iota(shape, 0), iota(shape, 1)
    below = row > lane
    above = row < lane

    def matrix(mask, yes, no):
        return jnp.where(mask, yes, no).astype(jnp.bfloat16)

    plain = ((1,), (0,))
    inputs, cotangent = both[0], both[1]
    total = dot(matrix(below, own_t, other), inputs, plain)
    total += dot(matrix(above, own_t, 0.0), left[0], plain)
    total += dot(matrix(below, other, 0.0), right[0], plain)
    mixed[...] = (total + own_first * inputs.astype(jnp.float32)).astype(jnp.bfloat16)
    total = dot(matrix(below, other_t, own), cotangent, plain)
    total += dot(matrix(below, own, 0.0), right[1], plain)
    total += dot(matrix(above, other_t, 0.0), left[1], plain)
    grad[...] = (total + other_first * cotangent.astype(jnp.float32)).astype(jnp.bfloat16)


def on_device(hidden, token_ids, embedding, filters, lengths, cotangent):
    shape = jax.ShapeDtypeStruct
    half = TAPS // 2
    symbols = pl.pallas_call(
        symbols_kernel,
        out_shape=shape((embedding.shape[0], ROWS), jnp.int32),
        in_specs=[],
        out_specs=VMEM,
        cost_estimate=cost(1 << 33, 1 << 24),
        compiler_params=ROOM,
    )()
    both = pl.pallas_call(
        inputs_kernel,
        out_shape=shape((2, ROWS, CHANS), jnp.bfloat16),
        in_specs=[VMEM] * 5,
        out_specs=VMEM,
        cost_estimate=cost(1, 1),
        compiler_params=ROOM,
    )(hidden, token_ids, embedding, cotangent, symbols)
    up = [(i, i + 1) for i in range(CTX_SIZE - 1)]
    left = lax.ppermute(both, CTX, up)
    right = lax.ppermute(both, CTX, [(j, i) for i, j in up])
    pair = (2, 8, ROWS)
    near = pl.pallas_call(
        near_kernel,
        out_shape=shape(pair, jnp.float32),
        in_specs=[VMEM],
        out_specs=VMEM,
        cost_estimate=cost(1, 1),
        compiler_params=ROOM,
    )(both)
    sums = pl.pallas_call(
        correlate_kernel,
        out_shape=shape((math.prod(SIZES[a] for a in FIRST), 4, half), jnp.float32),
        in_specs=[VMEM] * 3,
        out_specs=VMEM,
        cost_estimate=cost(1, 1),
        compiler_params=ROOM,
    )(both, right, near)
    sums = lax.all_to_all(sums, FIRST, 0, 0, axis_index_groups=[ORDER1])
    block = shape((ROWS, CHANS), jnp.bfloat16)
    mixed, hidden_grad, factor = pl.pallas_call(
        outputs_kernel,
        out_shape=(block, block, shape((GROUPS, TAPS), jnp.float32)),
        in_specs=[VMEM] * 4 + [SMEM],
        out_specs=(VMEM,) * 3,
        cost_estimate=cost(1, 1),
        compiler_params=ROOM,
    )(both, left, right, filters, lengths)
    sums, factor = lax.optimization_barrier((sums, factor))
    sums = pl.pallas_call(
        sum_kernel,
        out_shape=shape((math.prod(SIZES[a] for a in SECOND), len(kept_places()), 4, half), jnp.float32),
        in_specs=[VMEM],
        out_specs=VMEM,
        cost_estimate=cost(1, 1),
        compiler_params=ROOM,
    )(sums)
    sums = lax.all_to_all(sums, SECOND, 0, 0, axis_index_groups=[ORDER2])
    filter_grad = pl.pallas_call(
        finish_kernel,
        out_shape=shape((GROUPS, TAPS), jnp.float32),
        in_specs=[VMEM] * 2,
        out_specs=VMEM,
        cost_estimate=cost(1, 1),
        compiler_params=ROOM,
    )(sums, factor)
    return mixed, hidden_grad, filter_grad


def solution(mesh):
    names = tuple(name for name, _ in PARTS)
    fine = Mesh(mesh.devices.reshape([size for _, size in PARTS]), names)
    ctx, ch = names[:2], names[2:]
    placed = (P(ctx, ch), P(ctx), P(None, ch), P(), P(), P(ctx, ch))
    return jax.shard_map(
        on_device,
        mesh=fine,
        in_specs=placed,
        out_specs=(P(ctx, ch), P(ctx, ch), P()),
        check_vma=False,
    )
```
